32 devices in a mesh: groups: 2 (over y), docs: 8 (over z, x), rep: 2 (over core).
Axes of the slice: x: 2, y: 2, z: 4, core: 2. Of those that a mesh axis runs over, the one named last changes fastest.
Arguments:
- queries: bfloat16 [512, 32, 128], P(('groups', 'docs', 'rep')), parts along dimension 0, may hold values from -6 to 6
- candidates: int32 [512, 64], P(('groups', 'docs', 'rep')), parts along dimension 0, may hold values from 0 to 255, as said below
- doc_map: int32 [512], P('groups'), parts along dimension 0, may hold values from 0 to 255, as said below
- slabs: bfloat16 [512, 128, 128], P(('groups', 'docs')), parts along dimension 0, may hold values from -0.5 to 0.5
- doc_lengths: int32 [512], P(('groups', 'docs')), parts along dimension 0, may hold values from 16 to 128
Outputs:
- scores: float32 [512, 64], P(('groups', 'docs', 'rep')), parts along dimension 0
The draws below stay inside these ranges and needn't reach their ends.
There are 2 independent parts, one for each index of `groups`. The reference program is written for one: setup_inputs(seed, part) draws one part's arguments, and reference() takes and returns one part's arrays. A program takes and returns all parts, laid end to end along the dimension named above; each array names one. Nothing has to cross between parts.
Inputs may be any that keep to these rules, and one draw needn't show every extreme that they name: doc_map is a permutation: each row of slabs belongs to exactly one document id. A query's 64 candidates are distinct documents. Call doc_map[id] // 32 a document's owner: each query's candidates lie on exactly 8 owners, 8 on each. Of the 16 queries of one device at most 16 have candidates on any one owner, and in every draw some owners get exactly 16 queries from every device.
All inputs are finite; a program needn't handle non-finite values.
Results may differ from the reference program's by a relative error of at most 0.0003.
Values may be sent and summed in bfloat16 or wider, within the bound.
A program may use at most 64 MiB of HBM per device.

```python
import jax
import jax.numpy as jnp
from jax import lax

DIM = 128
QL = 32
DL = 128
SPREAD = 8
PER = 8
Q_DEV = 16
DOCS_DEV = 32
C = 64
CAP = 16
DOCS = 256
QUERIES = 256
N_DOCS = 8
N_REP = 2


def shared_layout(key):
    return jax.random.permutation(key, DOCS).astype(jnp.int32)


def distinct_order(key, shape, width):
    noise = jax.random.randint(key, shape, 0, 1 << 20).astype(jnp.int32)
    return jnp.argsort(noise * width + jnp.arange(width, dtype=jnp.int32), axis=-1, stable=True).astype(jnp.int32)


def draw_doc_map(key, part):
    layout = shared_layout(key)
    return layout


def draw_candidates(key, part):
    layout = shared_layout(key)
    key = jax.random.fold_in(key, 2)
    inverse = jnp.zeros((DOCS,), jnp.int32).at[layout].set(jnp.arange(DOCS, dtype=jnp.int32))
    sources = N_DOCS * N_REP
    step = N_DOCS // SPREAD
    seats = max(1, (step - 1) * CAP)
    key_hot, key_seat, key_shuffle, key_local, key_order = jax.random.split(key, 5)
    hot = jax.random.randint(key_hot, (), 0, step).astype(jnp.int32)
    seat_order = distinct_order(key_seat, (sources, seats), seats)
    others = seat_order[:, :Q_DEV - CAP]
    other_res = (hot + 1 + others // CAP) % step
    hot_res = jnp.zeros((sources, CAP), jnp.int32) + hot
    residues = jnp.concatenate([hot_res, other_res.astype(jnp.int32)], axis=1)
    shuffle = distinct_order(key_shuffle, (sources, Q_DEV), Q_DEV)
    residues = jnp.take_along_axis(residues, shuffle, axis=1)
    owners = residues[:, :, None] + step * jnp.arange(SPREAD, dtype=jnp.int32)[None, None, :]
    local_order = distinct_order(key_local, (sources, Q_DEV, SPREAD, DOCS_DEV), DOCS_DEV)[..., :PER]
    rows = owners[..., None] * DOCS_DEV + local_order
    rows = rows.reshape(QUERIES, C)
    column_order = distinct_order(key_order, (QUERIES, C), C)
    rows = jnp.take_along_axis(rows, column_order, axis=1)
    return jnp.take(inverse, rows).astype(jnp.int32)


def place_ends(array, own_key, least, largest):
    longest = array.shape.index(max(array.shape))
    spots = []
    for shift in (0, 1):
        where = [jax.random.randint(jax.random.fold_in(own_key, axis), (), 0, length) for axis, length in enumerate(array.shape)]
        where[longest] = (where[longest] + shift) % array.shape[longest]
        spots.append(tuple(where))
    return array.at[spots[0]].set(least).at[spots[1]].set(largest)


def levels(rng, shape, cuts, low, top_value):
    gain, own = 1.0, jax.random.fold_in(rng, 6)
    for dim, parts in cuts:
        draws = jnp.exp(jax.random.uniform(jax.random.fold_in(own, dim), (parts,), jnp.float32, low / len(cuts), top_value / len(cuts)))
        gain = gain * jnp.repeat(draws, shape[dim] // parts).reshape([-1 if axis == dim else 1 for axis in range(len(shape))])
    return gain


def bell_draw(stream_key, extent, deviation, limit, cuts=(), held_as=jnp.bfloat16):
    level = levels(stream_key, extent, cuts, -0.22, 0.18) if cuts else 1.0
    array = jax.random.normal(stream_key, extent, jnp.float32) * deviation * level
    return jnp.minimum(jnp.maximum(array, -limit), limit).astype(held_as)


def setup_inputs(seed: int = 0, part: int = 0) -> dict:
    keys = jax.random.split(jax.random.key(seed), 6)
    part_splits = jax.random.split(jax.random.fold_in(keys[5], part), 6)
    return {
        "queries": bell_draw(part_splits[0], (QUERIES, QL, DIM), 1.0, 6.0, ((0, 16),)),
        "candidates": draw_candidates(jax.random.fold_in(jax.random.fold_in(keys[5], part), 71), part),
        "doc_map": draw_doc_map(jax.random.fold_in(jax.random.fold_in(keys[5], part), 71), part),
        "slabs": bell_draw(part_splits[3], (DOCS, DL, DIM), DIM ** -0.5, 0.5, ((0, 8),)),
        "doc_lengths": place_ends(jax.random.randint(part_splits[4], (DOCS,), DL // 8, DL + 1), jax.random.fold_in(part_splits[4], 1), DL // 8, DL).astype(jnp.int32),
    }


def reference(queries, candidates, doc_map, slabs, doc_lengths):
    position = jnp.take(doc_map, candidates).astype(jnp.int32)
    token_ids = jnp.arange(DL, dtype=jnp.int32)

    def one_block(pieces):
        block_q, block_p = pieces
        docs = jnp.take(slabs, block_p, axis=0).astype(jnp.float32)
        lens = jnp.take(doc_lengths, block_p)
        dots = jnp.einsum("bik,bcjk->bcij", block_q.astype(jnp.float32), docs)
        alive = token_ids[None, None, None, :] < lens[:, :, None, None]
        best = jnp.max(jnp.where(alive, dots, -1e30), axis=3)
        return jnp.sum(best, axis=2) / QL

    blocks_q = queries.reshape(QUERIES // Q_DEV, Q_DEV, QL, DIM)
    blocks_p = position.reshape(QUERIES // Q_DEV, Q_DEV, C)
    result = lax.map(one_block, (blocks_q, blocks_p))
    return result.reshape(QUERIES, C)
```

```python
import math

import jax
import jax.numpy as jnp
from jax import lax
from jax.experimental import pallas as pl
from jax.experimental.pallas import tpu as pltpu
from jax.sharding import PartitionSpec as P

SPREAD = 8
PER = 8


def score_items(rows, wanted, slabs, doc_lengths):
    sources, items, qlen, dim = rows.shape
    docs_dev, dlen = (slabs.shape[0], slabs.shape[1])
    per = wanted.shape[2]
    group = math.gcd(sources, 16)
    token_ids = jnp.arange(dlen, dtype=jnp.int32)
    alive = token_ids[None, :] < doc_lengths[:, None]
    doc_ids = jnp.arange(docs_dev, dtype=jnp.int32)
    row_blocks = rows.reshape(sources // group, group * items, qlen, dim)
    want_blocks = wanted.reshape(sources // group, group * items, per)

    def one_block(block):
        block_rows, block_want = block
        dots = jnp.einsum("bik,djk->bidj", block_rows, slabs, preferred_element_type=jnp.float32)
        best = jnp.max(jnp.where(alive[None, None], dots, -1e30), axis=3)
        totals = jnp.sum(best, axis=1) / qlen
        match = block_want[:, :, None] == doc_ids[None, None, :]
        return jnp.sum(jnp.where(match, totals[:, None, :], 0.0), axis=2)

    result = lax.map(one_block, (row_blocks, want_blocks))
    return result.reshape(sources, items, per)


def body(queries, candidates, doc_map, slabs, doc_lengths):
    q_dev, qlen, dim = queries.shape
    docs_dev = slabs.shape[0]
    shards = lax.axis_size("docs")
    cands = candidates.shape[1]
    capacity = min(q_dev, max(2, 2 * q_dev * SPREAD // shards))
    position = jnp.take(doc_map, candidates)
    owner = position // docs_dev
    local = position % docs_dev
    shard_ids = jnp.arange(shards, dtype=jnp.int32)
    hits = jnp.any(owner[:, :, None] == shard_ids[None, None, :], axis=1)
    hit_count = hits.astype(jnp.int32)
    rank = jnp.cumsum(hit_count, axis=0) - hit_count
    seat_ids = jnp.arange(capacity, dtype=jnp.int32)
    select = hits[None, :, :] & (rank[None, :, :] == seat_ids[:, None, None])
    onehot = select.astype(jnp.bfloat16)
    outgoing = jnp.einsum(
        "cjs,jik->scik", onehot, queries, preferred_element_type=jnp.float32
    ).astype(jnp.bfloat16)
    slot = jnp.take_along_axis(rank, owner, axis=1)
    cand_ids = jnp.arange(cands, dtype=jnp.int32)
    same_owner = owner[:, :, None] == owner[:, None, :]
    earlier = cand_ids[None, :] < cand_ids[:, None]
    order = jnp.sum((same_owner & earlier[None]).astype(jnp.int32), axis=2)
    per_ids = jnp.arange(PER, dtype=jnp.int32)
    match = (owner[:, :, None, None] == shard_ids[None, None, :, None]) & (
        order[:, :, None, None] == per_ids[None, None, None, :]
    )
    listed = jnp.sum(jnp.where(match, local[:, :, None, None], 0), axis=1)
    picked = jnp.sum(jnp.where(select[:, :, :, None], listed[None], 0), axis=1)
    picked = jnp.transpose(picked, (1, 0, 2))
    arrived_rows, arrived_want = (
        lax.all_to_all(outgoing, "docs", split_axis=0, concat_axis=0, tiled=True),
        lax.all_to_all(picked, "docs", split_axis=0, concat_axis=0, tiled=True),
    )
    result = score_items(arrived_rows, arrived_want, slabs, doc_lengths)
    answers = lax.all_to_all(result, "docs", split_axis=0, concat_axis=0, tiled=True)
    flat_index = (owner * capacity + slot) * PER + order
    return jnp.take(answers.reshape(-1), flat_index)


NCH = 2
MESH = pl.DeviceIdType.MESH


def gather_score_kernel(q_ref, slab_ref, len_ref, out_ref, held, docs, best, parts, table,
                        send_sem, recv_sem, back_send, back_recv):
    me = lax.axis_index("docs")
    z, x = me // 2, me % 2
    h = z // 2
    mate = z * 2 + (1 - x)
    rows = q_ref.shape[0]
    step_rows = rows // NCH
    n_docs, dlen, dim = slab_ref.shape
    shards = held.shape[0]
    middle = jnp.logical_or(z == 1, z == 2)

    barrier = pltpu.get_barrier_semaphore()
    for k in range(1, shards):
        pl.semaphore_signal(barrier, inc=1, device_id={"docs": (me + k) % shards}, device_id_type=MESH)
    pl.semaphore_wait(barrier, shards - 1)

    def chunk(c):
        return pl.ds(c * step_rows, step_rows)

    def link(source, origin, c, kind, target):
        return pltpu.make_async_remote_copy(
            src_ref=source.at[chunk(c)],
            dst_ref=held.at[origin, chunk(c)],
            send_sem=send_sem.at[kind * NCH + c],
            recv_sem=recv_sem.at[origin * NCH + c],
            device_id={"docs": target},
            device_id_type=MESH,
        )

    inner = (z + 1 - 2 * h) * 2 + x
    outer = jnp.where(middle, z - 1 + 2 * h, 1 + h) * 2 + x
    for c in range(NCH):
        link(q_ref, me, c, 0, inner).start()
        link(q_ref, me, c, 1, mate).start()

        @pl.when(middle)
        def _(c=c):
            link(q_ref, me, c, 2, outer).start()

    def mask_doc(d, carry):
        rows_d = slab_ref[d].astype(jnp.float32)
        live = lax.broadcasted_iota(jnp.int32, (dlen, dim), 0) < len_ref[d]
        docs[d] = jnp.where(live, rows_d, rows_d[0:1]).astype(jnp.bfloat16)
        return carry

    lax.fori_loop(0, n_docs, mask_doc, 0)

    col_q = lax.broadcasted_iota(jnp.int32, (16, rows), 1) // 32
    row_q = lax.broadcasted_iota(jnp.int32, (16, rows), 0)
    pick = jnp.where(col_q == row_q, 1.0, 0.0).astype(jnp.bfloat16)
    G = 8

    def score(source):
        q = source[...]

        def group(g, carry):
            block = docs[pl.ds(g * G, G)].reshape(G * dlen, dim)
            dots = lax.dot_general(block, q, (((1,), (1,)), ((), ())), preferred_element_type=jnp.float32)
            best[pl.ds(pl.multiple_of(g * G, G), G), :] = jnp.max(dots.reshape(G, dlen, rows), axis=1)
            return carry

        lax.fori_loop(0, n_docs // G, group, 0)
        full = best[...]
        hi = full.astype(jnp.bfloat16)
        rest = full - hi.astype(jnp.float32)
        mid = rest.astype(jnp.bfloat16)
        low = (rest - mid.astype(jnp.float32)).astype(jnp.bfloat16)
        stacked = jnp.concatenate([hi, mid, low, jnp.zeros_like(hi)], axis=0)
        total = lax.dot_general(pick, stacked, (((1,), (1,)), ((), ())), preferred_element_type=jnp.float32)
        return total * (1.0 / 32.0)

    def back(origin):
        return pltpu.make_async_remote_copy(
            src_ref=parts.at[origin],
            dst_ref=table.at[me],
            send_sem=back_send.at[origin],
            recv_sem=back_recv.at[me],
            device_id={"docs": origin},
            device_id_type=MESH,
        )

    def answer(origin):
        parts[origin] = score(held.at[origin])
        back(origin).start()

    def arrive(origin):
        for c in range(NCH):
            link(held.at[origin], origin, c, 0, mate).wait_recv()

    column = (1 - z + 4 * h, 2 - h, 3 - 3 * h)
    onward = jnp.where(middle, 3 - z, mate // 2), jnp.where(middle, 3 * h, mate // 2), jnp.where(middle, 3 * h, mate // 2)

    def relay(p, go):
        origin = column[p] * 2 + x
        target = jnp.where(middle, onward[p] * 2 + x, mate)
        for c in range(NCH):
            if go:
                link(held.at[origin], origin, c, 0, mate).wait_recv()

            @pl.when(middle)
            def _(c=c):
                out = link(held.at[origin], origin, c, 3 + 2 * p, target)
                out.start() if go else out.wait_send()

            out = link(held.at[origin], origin, c, 4 + 2 * p, mate)
            out.start() if go else out.wait_send()
        return origin

    table[me] = score(q_ref)
    first = relay(0, True)
    answer(first)
    arrive(mate)
    answer(mate)
    second = relay(1, True)
    answer(second)
    arrive(column[0] * 2 + 1 - x)
    answer(column[0] * 2 + 1 - x)
    third = relay(2, True)
    answer(third)
    for p in (1, 2):
        arrive(column[p] * 2 + 1 - x)
        answer(column[p] * 2 + 1 - x)

    for c in range(NCH):
        link(q_ref, me, c, 0, inner).wait_send()
        link(q_ref, me, c, 1, mate).wait_send()

        @pl.when(middle)
        def _(c=c):
            link(q_ref, me, c, 2, outer).wait_send()
    for p in range(3):
        relay(p, False)
    for k in range(1, shards):
        other = (me + k) % shards
        back(other).wait_send()
        pltpu.make_async_remote_copy(
            src_ref=parts.at[other], dst_ref=table.at[other], send_sem=back_send.at[other],
            recv_sem=back_recv.at[other], device_id={"docs": other}, device_id_type=MESH,
        ).wait_recv()
    out_ref[...] = table[...]


def pick_kernel(table_ref, cand_ref, map_ref, out_ref):
    cand = cand_ref[...]
    items, cands = cand.shape
    lanes = 128
    cand = jnp.concatenate([cand, cand], axis=1)
    low = cand % lanes
    position = jnp.zeros_like(cand)
    for b in range(map_ref.shape[1] // lanes):
        piece = jnp.broadcast_to(map_ref[:, b * lanes:(b + 1) * lanes], (items, lanes))
        got = jnp.take_along_axis(piece, low, axis=1)
        position = jnp.where(cand // lanes == b, got, position)
    owner, local = position // 32, position % 32
    out = jnp.zeros((items, lanes), jnp.float32)
    for o in range(table_ref.shape[0]):
        part = table_ref[o]
        got = (jnp.take_along_axis(part, local, axis=1) + jnp.take_along_axis(part, local + 32, axis=1)
               + jnp.take_along_axis(part, local + 64, axis=1))
        out = jnp.where(owner == o, got, out)
    out_ref[...] = out[:, :cands]


def dense_body(queries, candidates, doc_map, slabs, doc_lengths):
    q_dev, qlen, dim = queries.shape
    shards = lax.axis_size("docs")
    rows = q_dev * qlen
    vmem = pl.BlockSpec(memory_space=pltpu.VMEM)
    table = pl.pallas_call(
        gather_score_kernel,
        out_shape=jax.ShapeDtypeStruct((shards, q_dev, 128), jnp.float32),
        in_specs=[vmem, vmem, pl.BlockSpec(memory_space=pltpu.SMEM)],
        out_specs=vmem,
        scratch_shapes=[
            pltpu.VMEM((shards, rows, dim), jnp.bfloat16),
            pltpu.VMEM(slabs.shape, jnp.bfloat16),
            pltpu.VMEM((slabs.shape[0], rows), jnp.float32),
            pltpu.VMEM((shards, q_dev, 128), jnp.float32),
            pltpu.VMEM((shards, q_dev, 128), jnp.float32),
            pltpu.SemaphoreType.DMA((9 * NCH,)),
            pltpu.SemaphoreType.DMA((shards * NCH,)),
            pltpu.SemaphoreType.DMA((shards,)),
            pltpu.SemaphoreType.DMA((shards,)),
        ],
        compiler_params=pltpu.CompilerParams(
            collective_id=0, has_side_effects=True, vmem_limit_bytes=40 * 1024 * 1024
        ),
        name="gather_score",
    )(queries.reshape(rows, dim), slabs, doc_lengths)
    return pl.pallas_call(
        pick_kernel,
        out_shape=jax.ShapeDtypeStruct(candidates.shape, jnp.float32),
        in_specs=[vmem] * 3,
        out_specs=vmem,
        name="pick",
    )(table, candidates, doc_map.reshape(1, -1))


def any_body(queries, candidates, doc_map, slabs, doc_lengths):
    sizes = (queries.shape, candidates.shape, slabs.shape, lax.axis_size("docs"))
    if sizes == ((16, 32, 128), (16, 64), (32, 128, 128), 8):
        return dense_body(queries, candidates, doc_map, slabs, doc_lengths)
    return body(queries, candidates, doc_map, slabs, doc_lengths)


def solution(mesh):
    placed = (
        P(("groups", "docs", "rep"), None, None),
        P(("groups", "docs", "rep"), None),
        P("groups"),
        P(("groups", "docs"), None, None),
        P(("groups", "docs")),
    )
    return jax.shard_map(
        any_body,
        mesh=mesh,
        in_specs=placed,
        out_specs=P(("groups", "docs", "rep"), None),
        check_vma=False,
    )
```

```python
import math

import jax
import jax.numpy as jnp
from jax import lax
from jax.experimental import pallas as pl
from jax.experimental.pallas import tpu as pltpu
from jax.sharding import PartitionSpec as P

SPREAD = 8
PER = 8


def score_items(rows, wanted, slabs, doc_lengths):
    sources, items, qlen, dim = rows.shape
    docs_dev, dlen = (slabs.shape[0], slabs.shape[1])
    per = wanted.shape[2]
    group = math.gcd(sources, 16)
    token_ids = jnp.arange(dlen, dtype=jnp.int32)
    alive = token_ids[None, :] < doc_lengths[:, None]
    doc_ids = jnp.arange(docs_dev, dtype=jnp.int32)
    row_blocks = rows.reshape(sources // group, group * items, qlen, dim)
    want_blocks = wanted.reshape(sources // group, group * items, per)

    def one_block(block):
        block_rows, block_want = block
        dots = jnp.einsum("bik,djk->bidj", block_rows, slabs, preferred_element_type=jnp.float32)
        best = jnp.max(jnp.where(alive[None, None], dots, -1e30), axis=3)
        totals = jnp.sum(best, axis=1) / qlen
        match = block_want[:, :, None] == doc_ids[None, None, :]
        return jnp.sum(jnp.where(match, totals[:, None, :], 0.0), axis=2)

    result = lax.map(one_block, (row_blocks, want_blocks))
    return result.reshape(sources, items, per)


def body(queries, candidates, doc_map, slabs, doc_lengths):
    q_dev, qlen, dim = queries.shape
    docs_dev = slabs.shape[0]
    shards = lax.axis_size("docs")
    cands = candidates.shape[1]
    capacity = min(q_dev, max(2, 2 * q_dev * SPREAD // shards))
    position = jnp.take(doc_map, candidates)
    owner = position // docs_dev
    local = position % docs_dev
    shard_ids = jnp.arange(shards, dtype=jnp.int32)
    hits = jnp.any(owner[:, :, None] == shard_ids[None, None, :], axis=1)
    hit_count = hits.astype(jnp.int32)
    rank = jnp.cumsum(hit_count, axis=0) - hit_count
    seat_ids = jnp.arange(capacity, dtype=jnp.int32)
    select = hits[None, :, :] & (rank[None, :, :] == seat_ids[:, None, None])
    onehot = select.astype(jnp.bfloat16)
    outgoing = jnp.einsum(
        "cjs,jik->scik", onehot, queries, preferred_element_type=jnp.float32
    ).astype(jnp.bfloat16)
    slot = jnp.take_along_axis(rank, owner, axis=1)
    cand_ids = jnp.arange(cands, dtype=jnp.int32)
    same_owner = owner[:, :, None] == owner[:, None, :]
    earlier = cand_ids[None, :] < cand_ids[:, None]
    order = jnp.sum((same_owner & earlier[None]).astype(jnp.int32), axis=2)
    per_ids = jnp.arange(PER, dtype=jnp.int32)
    match = (owner[:, :, None, None] == shard_ids[None, None, :, None]) & (
        order[:, :, None, None] == per_ids[None, None, None, :]
    )
    listed = jnp.sum(jnp.where(match, local[:, :, None, None], 0), axis=1)
    picked = jnp.sum(jnp.where(select[:, :, :, None], listed[None], 0), axis=1)
    picked = jnp.transpose(picked, (1, 0, 2))
    arrived_rows, arrived_want = (
        lax.all_to_all(outgoing, "docs", split_axis=0, concat_axis=0, tiled=True),
        lax.all_to_all(picked, "docs", split_axis=0, concat_axis=0, tiled=True),
    )
    result = score_items(arrived_rows, arrived_want, slabs, doc_lengths)
    answers = lax.all_to_all(result, "docs", split_axis=0, concat_axis=0, tiled=True)
    flat_index = (owner * capacity + slot) * PER + order
    return jnp.take(answers.reshape(-1), flat_index)


NCH = 2
MESH = pl.DeviceIdType.MESH


def gather_score_kernel(q_ref, slab_ref, len_hbm, cand_hbm, map_hbm, out_ref, held, docs, best, parts, table,
                        len_ref, cand_ref, map_ref, send_sem, recv_sem, back_send, back_recv, load_sem):
    me = lax.axis_index("docs")
    z, x = me // 2, me % 2
    h = z // 2
    mate = z * 2 + (1 - x)
    rows = q_ref.shape[0]
    step_rows = rows // NCH
    n_docs, dlen, dim = slab_ref.shape
    shards = held.shape[0]
    loads = [
        pltpu.make_async_copy(src, dst, load_sem.at[i])
        for i, (src, dst) in enumerate((
            (slab_ref, docs), (len_hbm, len_ref), (q_ref, held.at[me]), (cand_hbm, cand_ref), (map_hbm, map_ref)))
    ]
    middle = jnp.logical_or(z == 1, z == 2)

    barrier = pltpu.get_barrier_semaphore()
    for k in range(1, shards):
        pl.semaphore_signal(barrier, inc=1, device_id={"docs": (me + k) % shards}, device_id_type=MESH)
    for load in loads:
        load.start()
    pl.semaphore_wait(barrier, shards - 1)

    def chunk(c):
        return pl.ds(c * step_rows, step_rows)

    def link(source, origin, c, kind, target):
        return pltpu.make_async_remote_copy(
            src_ref=source.at[chunk(c)],
            dst_ref=held.at[origin, chunk(c)],
            send_sem=send_sem.at[kind * NCH + c],
            recv_sem=recv_sem.at[origin * NCH + c],
            device_id={"docs": target},
            device_id_type=MESH,
        )

    inner = (z + 1 - 2 * h) * 2 + x
    outer = jnp.where(middle, z - 1 + 2 * h, 1 + h) * 2 + x
    for c in range(NCH):
        link(q_ref, me, c, 0, inner).start()
        link(q_ref, me, c, 1, mate).start()

        @pl.when(middle)
        def _(c=c):
            link(q_ref, me, c, 2, outer).start()

    loads[0].wait()
    loads[1].wait()

    def mask_doc(d, carry):
        rows_d = docs[d].astype(jnp.float32)
        live = lax.broadcasted_iota(jnp.int32, (dlen, dim), 0) < len_ref[d]
        docs[d] = jnp.where(live, rows_d, rows_d[0:1]).astype(jnp.bfloat16)
        return carry

    lax.fori_loop(0, n_docs, mask_doc, 0, unroll=2)

    col_q = lax.broadcasted_iota(jnp.int32, (16, rows), 1) // 32
    row_q = lax.broadcasted_iota(jnp.int32, (16, rows), 0)
    pick = jnp.where(col_q == row_q, 1.0, 0.0).astype(jnp.bfloat16)
    G = 8

    def score(source):
        q = source[...]

        def group(g, carry):
            block = docs[pl.ds(g * G, G)].reshape(G * dlen, dim)
            dots = lax.dot_general(block, q, (((1,), (1,)), ((), ())), preferred_element_type=jnp.float32)
            best[pl.ds(pl.multiple_of(g * G, G), G), :] = jnp.max(dots.reshape(G, dlen, rows), axis=1)
            return carry

        lax.fori_loop(0, n_docs // G, group, 0, unroll=True)
        full = best[...]
        hi = full.astype(jnp.bfloat16)
        rest = full - hi.astype(jnp.float32)
        mid = rest.astype(jnp.bfloat16)
        low = (rest - mid.astype(jnp.float32)).astype(jnp.bfloat16)
        stacked = jnp.concatenate([hi, mid, low, jnp.zeros_like(hi)], axis=0)
        total = lax.dot_general(pick, stacked, (((1,), (1,)), ((), ())), preferred_element_type=jnp.float32)
        return total * (1.0 / 32.0)

    def back(origin):
        return pltpu.make_async_remote_copy(
            src_ref=parts.at[origin],
            dst_ref=table.at[me],
            send_sem=back_send.at[origin],
            recv_sem=back_recv.at[me],
            device_id={"docs": origin},
            device_id_type=MESH,
        )

    def answer(origin):
        parts[origin] = score(held.at[origin])
        back(origin).start()

    def arrive(origin):
        for c in range(NCH):
            link(held.at[origin], origin, c, 0, mate).wait_recv()

    column = (1 - z + 4 * h, 2 - h, 3 - 3 * h)
    onward = jnp.where(middle, 3 - z, mate // 2), jnp.where(middle, 3 * h, mate // 2), jnp.where(middle, 3 * h, mate // 2)

    def relay(p, go):
        origin = column[p] * 2 + x
        target = jnp.where(middle, onward[p] * 2 + x, mate)
        for c in range(NCH):
            if go:
                link(held.at[origin], origin, c, 0, mate).wait_recv()

            @pl.when(middle)
            def _(c=c):
                out = link(held.at[origin], origin, c, 3 + 2 * p, target)
                out.start() if go else out.wait_send()

            out = link(held.at[origin], origin, c, 4 + 2 * p, mate)
            out.start() if go else out.wait_send()
        return origin

    loads[2].wait()
    table[me] = score(held.at[me])
    first = relay(0, True)
    answer(first)
    arrive(mate)
    answer(mate)
    second = relay(1, True)
    answer(second)
    arrive(column[0] * 2 + 1 - x)
    answer(column[0] * 2 + 1 - x)
    third = relay(2, True)
    answer(third)
    for p in (1, 2):
        arrive(column[p] * 2 + 1 - x)
        answer(column[p] * 2 + 1 - x)

    for c in range(NCH):
        link(q_ref, me, c, 0, inner).wait_send()
        link(q_ref, me, c, 1, mate).wait_send()

        @pl.when(middle)
        def _(c=c):
            link(q_ref, me, c, 2, outer).wait_send()
    for p in range(3):
        relay(p, False)
    for k in range(1, shards):
        other = (me + k) % shards
        back(other).wait_send()
        pltpu.make_async_remote_copy(
            src_ref=parts.at[other], dst_ref=table.at[other], send_sem=back_send.at[other],
            recv_sem=back_recv.at[other], device_id={"docs": other}, device_id_type=MESH,
        ).wait_recv()
    loads[3].wait()
    loads[4].wait()
    cand = cand_ref[...]
    items, cands = cand.shape
    lanes = 128
    cand = jnp.concatenate([cand, cand], axis=1)
    low = cand % lanes
    position = jnp.zeros_like(cand)
    for b in range(map_ref.shape[1] // lanes):
        piece = jnp.broadcast_to(map_ref[:, b * lanes:(b + 1) * lanes], (items, lanes))
        got = jnp.take_along_axis(piece, low, axis=1)
        position = jnp.where(cand // lanes == b, got, position)
    owner, local = position // 32, position % 32
    out = jnp.zeros((items, lanes), jnp.float32)
    for o in range(shards):
        part = table[o]
        got = (jnp.take_along_axis(part, local, axis=1) + jnp.take_along_axis(part, local + 32, axis=1)
               + jnp.take_along_axis(part, local + 64, axis=1))
        out = jnp.where(owner == o, got, out)
    out_ref[...] = out[:, :cands]


def dense_body(queries, candidates, doc_map, slabs, doc_lengths):
    q_dev, qlen, dim = queries.shape
    shards = lax.axis_size("docs")
    rows = q_dev * qlen
    vmem = pl.BlockSpec(memory_space=pltpu.VMEM)
    hbm = pl.BlockSpec(memory_space=pl.ANY)
    return pl.pallas_call(
        gather_score_kernel,
        out_shape=jax.ShapeDtypeStruct(candidates.shape, jnp.float32),
        in_specs=[hbm] * 5,
        out_specs=vmem,
        scratch_shapes=[
            pltpu.VMEM((shards, rows, dim), jnp.bfloat16),
            pltpu.VMEM(slabs.shape, jnp.bfloat16),
            pltpu.VMEM((slabs.shape[0], rows), jnp.float32),
            pltpu.VMEM((shards, q_dev, 128), jnp.float32),
            pltpu.VMEM((shards, q_dev, 128), jnp.float32),
            pltpu.SMEM(doc_lengths.shape, jnp.int32),
            pltpu.VMEM(candidates.shape, jnp.int32),
            pltpu.VMEM((1,) + doc_map.shape, jnp.int32),
            pltpu.SemaphoreType.DMA((9 * NCH,)),
            pltpu.SemaphoreType.DMA((shards * NCH,)),
            pltpu.SemaphoreType.DMA((shards,)),
            pltpu.SemaphoreType.DMA((shards,)),
            pltpu.SemaphoreType.DMA((5,)),
        ],
        compiler_params=pltpu.CompilerParams(
            collective_id=0, has_side_effects=True, vmem_limit_bytes=60 * 1024 * 1024
        ),
        name="gather_score",
    )(queries.reshape(rows, dim), slabs, doc_lengths, candidates, doc_map.reshape(1, -1))


def any_body(queries, candidates, doc_map, slabs, doc_lengths):
    sizes = (queries.shape, candidates.shape, slabs.shape, lax.axis_size("docs"))
    if sizes == ((16, 32, 128), (16, 64), (32, 128, 128), 8):
        return dense_body(queries, candidates, doc_map, slabs, doc_lengths)
    return body(queries, candidates, doc_map, slabs, doc_lengths)


def solution(mesh):
    placed = (
        P(("groups", "docs", "rep"), None, None),
        P(("groups", "docs", "rep"), None),
        P("groups"),
        P(("groups", "docs"), None, None),
        P(("groups", "docs")),
    )
    return jax.shard_map(
        any_body,
        mesh=mesh,
        in_specs=placed,
        out_specs=P(("groups", "docs", "rep"), None),
        check_vma=False,
    )
```

```python
import math

import jax
import jax.numpy as jnp
from jax import lax
from jax.experimental import pallas as pl
from jax.experimental.pallas import tpu as pltpu
from jax.sharding import PartitionSpec as P

SPREAD = 8
PER = 8


def score_items(rows, wanted, slabs, doc_lengths):
    sources, items, qlen, dim = rows.shape
    docs_dev, dlen = (slabs.shape[0], slabs.shape[1])
    per = wanted.shape[2]
    group = math.gcd(sources, 16)
    token_ids = jnp.arange(dlen, dtype=jnp.int32)
    alive = token_ids[None, :] < doc_lengths[:, None]
    doc_ids = jnp.arange(docs_dev, dtype=jnp.int32)
    row_blocks = rows.reshape(sources // group, group * items, qlen, dim)
    want_blocks = wanted.reshape(sources // group, group * items, per)

    def one_block(block):
        block_rows, block_want = block
        dots = jnp.einsum("bik,djk->bidj", block_rows, slabs, preferred_element_type=jnp.float32)
        best = jnp.max(jnp.where(alive[None, None], dots, -1e30), axis=3)
        totals = jnp.sum(best, axis=1) / qlen
        match = block_want[:, :, None] == doc_ids[None, None, :]
        return jnp.sum(jnp.where(match, totals[:, None, :], 0.0), axis=2)

    result = lax.map(one_block, (row_blocks, want_blocks))
    return result.reshape(sources, items, per)


def body(queries, candidates, doc_map, slabs, doc_lengths):
    q_dev, qlen, dim = queries.shape
    docs_dev = slabs.shape[0]
    shards = lax.axis_size("docs")
    cands = candidates.shape[1]
    capacity = min(q_dev, max(2, 2 * q_dev * SPREAD // shards))
    position = jnp.take(doc_map, candidates)
    owner = position // docs_dev
    local = position % docs_dev
    shard_ids = jnp.arange(shards, dtype=jnp.int32)
    hits = jnp.any(owner[:, :, None] == shard_ids[None, None, :], axis=1)
    hit_count = hits.astype(jnp.int32)
    rank = jnp.cumsum(hit_count, axis=0) - hit_count
    seat_ids = jnp.arange(capacity, dtype=jnp.int32)
    select = hits[None, :, :] & (rank[None, :, :] == seat_ids[:, None, None])
    onehot = select.astype(jnp.bfloat16)
    outgoing = jnp.einsum(
        "cjs,jik->scik", onehot, queries, preferred_element_type=jnp.float32
    ).astype(jnp.bfloat16)
    slot = jnp.take_along_axis(rank, owner, axis=1)
    cand_ids = jnp.arange(cands, dtype=jnp.int32)
    same_owner = owner[:, :, None] == owner[:, None, :]
    earlier = cand_ids[None, :] < cand_ids[:, None]
    order = jnp.sum((same_owner & earlier[None]).astype(jnp.int32), axis=2)
    per_ids = jnp.arange(PER, dtype=jnp.int32)
    match = (owner[:, :, None, None] == shard_ids[None, None, :, None]) & (
        order[:, :, None, None] == per_ids[None, None, None, :]
    )
    listed = jnp.sum(jnp.where(match, local[:, :, None, None], 0), axis=1)
    picked = jnp.sum(jnp.where(select[:, :, :, None], listed[None], 0), axis=1)
    picked = jnp.transpose(picked, (1, 0, 2))
    arrived_rows, arrived_want = (
        lax.all_to_all(outgoing, "docs", split_axis=0, concat_axis=0, tiled=True),
        lax.all_to_all(picked, "docs", split_axis=0, concat_axis=0, tiled=True),
    )
    result = score_items(arrived_rows, arrived_want, slabs, doc_lengths)
    answers = lax.all_to_all(result, "docs", split_axis=0, concat_axis=0, tiled=True)
    flat_index = (owner * capacity + slot) * PER + order
    return jnp.take(answers.reshape(-1), flat_index)


NCH = 2
MESH = pl.DeviceIdType.MESH


def gather_score_kernel(q_ref, slab_ref, len_hbm, cand_hbm, map_hbm, out_ref, held, docs, best, parts, table,
                        len_ref, cand_ref, map_ref, send_sem, recv_sem, back_send, back_recv, load_sem):
    me = lax.axis_index("docs")
    z, x = me // 2, me % 2
    h = z // 2
    mate = z * 2 + (1 - x)
    rows = q_ref.shape[0]
    step_rows = rows // NCH
    n_docs, dlen, dim = slab_ref.shape
    shards = held.shape[0]
    loads = [
        pltpu.make_async_copy(src, dst, load_sem.at[i])
        for i, (src, dst) in enumerate((
            (slab_ref, docs), (len_hbm, len_ref), (q_ref, held.at[me]), (cand_hbm, cand_ref), (map_hbm, map_ref)))
    ]
    middle = jnp.logical_or(z == 1, z == 2)

    barrier = pltpu.get_barrier_semaphore()
    for k in range(1, shards):
        pl.semaphore_signal(barrier, inc=1, device_id={"docs": (me + k) % shards}, device_id_type=MESH)
    for load in loads:
        load.start()
    pl.semaphore_wait(barrier, shards - 1)

    def chunk(c):
        return pl.ds(c * step_rows, step_rows)

    def link(source, origin, c, kind, target):
        return pltpu.make_async_remote_copy(
            src_ref=source.at[chunk(c)],
            dst_ref=held.at[origin, chunk(c)],
            send_sem=send_sem.at[kind * NCH + c],
            recv_sem=recv_sem.at[origin * NCH + c],
            device_id={"docs": target},
            device_id_type=MESH,
        )

    inner = (z + 1 - 2 * h) * 2 + x
    outer = jnp.where(middle, z - 1 + 2 * h, 1 + h) * 2 + x
    for c in range(NCH):
        link(q_ref, me, c, 0, inner).start()
        link(q_ref, me, c, 1, mate).start()

        @pl.when(middle)
        def _(c=c):
            link(q_ref, me, c, 2, outer).start()

    loads[0].wait()
    loads[1].wait()

    def mask_doc(d, carry):
        rows_d = docs[d].astype(jnp.float32)
        live = lax.broadcasted_iota(jnp.int32, (dlen, dim), 0) < len_ref[d]
        docs[d] = jnp.where(live, rows_d, rows_d[0:1]).astype(jnp.bfloat16)
        return carry

    lax.fori_loop(0, n_docs, mask_doc, 0, unroll=2)

    col_q = lax.broadcasted_iota(jnp.int32, (16, rows), 1) // 32
    row_q = lax.broadcasted_iota(jnp.int32, (16, rows), 0)
    pick = jnp.where(col_q == row_q, 1.0, 0.0).astype(jnp.bfloat16)
    G = 8

    def half(origin, c):
        q = held[origin, chunk(c)]

        def group(g, carry):
            block = docs[pl.ds(g * G, G)].reshape(G * dlen, dim)
            dots = lax.dot_general(block, q, (((1,), (1,)), ((), ())), preferred_element_type=jnp.float32)
            best[pl.ds(pl.multiple_of(g * G, G), G), chunk(c)] = jnp.max(
                dots.reshape(G, dlen, step_rows), axis=1)
            return carry

        lax.fori_loop(0, n_docs // G, group, 0, unroll=True)

    def total():
        full = best[...]
        hi = full.astype(jnp.bfloat16)
        rest = full - hi.astype(jnp.float32)
        mid = rest.astype(jnp.bfloat16)
        low = (rest - mid.astype(jnp.float32)).astype(jnp.bfloat16)
        stacked = jnp.concatenate([hi, mid, low, jnp.zeros_like(hi)], axis=0)
        summed = lax.dot_general(pick, stacked, (((1,), (1,)), ((), ())), preferred_element_type=jnp.float32)
        return summed * (1.0 / 32.0)

    def back(origin):
        return pltpu.make_async_remote_copy(
            src_ref=parts.at[origin],
            dst_ref=table.at[me],
            send_sem=back_send.at[origin],
            recv_sem=back_recv.at[me],
            device_id={"docs": origin},
            device_id_type=MESH,
        )

    def answer(origin):
        parts[origin] = total()
        back(origin).start()

    def arrive(origin, c):
        link(held.at[origin], origin, c, 0, mate).wait_recv()

    column = (1 - z + 4 * h, 2 - h, 3 - 3 * h)
    onward = jnp.where(middle, 3 - z, mate // 2), jnp.where(middle, 3 * h, mate // 2), jnp.where(middle, 3 * h, mate // 2)

    def relay(p, c, go=True):
        origin = column[p] * 2 + x
        target = jnp.where(middle, onward[p] * 2 + x, mate)
        if go:
            arrive(origin, c)

        side = link(held.at[origin], origin, c, 4 + 2 * p, mate)
        ahead = link(held.at[origin], origin, c, 3 + 2 * p, target)

        @pl.when(middle)
        def _():
            ahead.start() if go else ahead.wait_send()

        side.start() if go else side.wait_send()

    near = [column[p] * 2 + x for p in range(3)]
    far = [column[p] * 2 + 1 - x for p in range(3)]

    loads[2].wait()
    half(me, 0)
    relay(0, 0)
    half(me, 1)
    table[me] = total()
    relay(0, 1)
    half(near[0], 0)
    half(near[0], 1)
    answer(near[0])
    arrive(mate, 0)
    half(mate, 0)
    relay(1, 0)
    arrive(mate, 1)
    half(mate, 1)
    answer(mate)
    relay(1, 1)
    half(near[1], 0)
    half(near[1], 1)
    answer(near[1])
    arrive(far[0], 0)
    half(far[0], 0)
    relay(2, 0)
    arrive(far[0], 1)
    half(far[0], 1)
    answer(far[0])
    relay(2, 1)
    half(near[2], 0)
    half(near[2], 1)
    answer(near[2])
    for p in (1, 2):
        for c in range(NCH):
            arrive(far[p], c)
            half(far[p], c)
        answer(far[p])

    for c in range(NCH):
        link(q_ref, me, c, 0, inner).wait_send()
        link(q_ref, me, c, 1, mate).wait_send()

        @pl.when(middle)
        def _(c=c):
            link(q_ref, me, c, 2, outer).wait_send()
    for p in range(3):
        for c in range(NCH):
            relay(p, c, False)
    for k in range(1, shards):
        other = (me + k) % shards
        back(other).wait_send()
        pltpu.make_async_remote_copy(
            src_ref=parts.at[other], dst_ref=table.at[other], send_sem=back_send.at[other],
            recv_sem=back_recv.at[other], device_id={"docs": other}, device_id_type=MESH,
        ).wait_recv()
    loads[3].wait()
    loads[4].wait()
    cand = cand_ref[...]
    items, cands = cand.shape
    lanes = 128
    cand = jnp.concatenate([cand, cand], axis=1)
    low = cand % lanes
    position = jnp.zeros_like(cand)
    for b in range(map_ref.shape[1] // lanes):
        piece = jnp.broadcast_to(map_ref[:, b * lanes:(b + 1) * lanes], (items, lanes))
        got = jnp.take_along_axis(piece, low, axis=1)
        position = jnp.where(cand // lanes == b, got, position)
    owner, local = position // 32, position % 32
    out = jnp.zeros((items, lanes), jnp.float32)
    for o in range(shards):
        part = table[o]
        got = (jnp.take_along_axis(part, local, axis=1) + jnp.take_along_axis(part, local + 32, axis=1)
               + jnp.take_along_axis(part, local + 64, axis=1))
        out = jnp.where(owner == o, got, out)
    out_ref[...] = out[:, :cands]


def dense_body(queries, candidates, doc_map, slabs, doc_lengths):
    q_dev, qlen, dim = queries.shape
    shards = lax.axis_size("docs")
    rows = q_dev * qlen
    vmem = pl.BlockSpec(memory_space=pltpu.VMEM)
    hbm = pl.BlockSpec(memory_space=pl.ANY)
    return pl.pallas_call(
        gather_score_kernel,
        out_shape=jax.ShapeDtypeStruct(candidates.shape, jnp.float32),
        in_specs=[hbm] * 5,
        out_specs=vmem,
        scratch_shapes=[
            pltpu.VMEM((shards, rows, dim), jnp.bfloat16),
            pltpu.VMEM(slabs.shape, jnp.bfloat16),
            pltpu.VMEM((slabs.shape[0], rows), jnp.float32),
            pltpu.VMEM((shards, q_dev, 128), jnp.float32),
            pltpu.VMEM((shards, q_dev, 128), jnp.float32),
            pltpu.SMEM(doc_lengths.shape, jnp.int32),
            pltpu.VMEM(candidates.shape, jnp.int32),
            pltpu.VMEM((1,) + doc_map.shape, jnp.int32),
            pltpu.SemaphoreType.DMA((9 * NCH,)),
            pltpu.SemaphoreType.DMA((shards * NCH,)),
            pltpu.SemaphoreType.DMA((shards,)),
            pltpu.SemaphoreType.DMA((shards,)),
            pltpu.SemaphoreType.DMA((5,)),
        ],
        compiler_params=pltpu.CompilerParams(
            collective_id=0, has_side_effects=True, vmem_limit_bytes=60 * 1024 * 1024
        ),
        name="gather_score",
    )(queries.reshape(rows, dim), slabs, doc_lengths, candidates, doc_map.reshape(1, -1))


def any_body(queries, candidates, doc_map, slabs, doc_lengths):
    sizes = (queries.shape, candidates.shape, slabs.shape, lax.axis_size("docs"))
    if sizes == ((16, 32, 128), (16, 64), (32, 128, 128), 8):
        return dense_body(queries, candidates, doc_map, slabs, doc_lengths)
    return body(queries, candidates, doc_map, slabs, doc_lengths)


def solution(mesh):
    placed = (
        P(("groups", "docs", "rep"), None, None),
        P(("groups", "docs", "rep"), None),
        P("groups"),
        P(("groups", "docs"), None, None),
        P(("groups", "docs")),
    )
    return jax.shard_map(
        any_body,
        mesh=mesh,
        in_specs=placed,
        out_specs=P(("groups", "docs", "rep"), None),
        check_vma=False,
    )
```

```python
import math

import jax
import jax.numpy as jnp
from jax import lax
from jax.experimental import pallas as pl
from jax.experimental.pallas import tpu as pltpu
from jax.sharding import PartitionSpec as P

SPREAD = 8
PER = 8


def score_items(rows, wanted, slabs, doc_lengths):
    sources, items, qlen, dim = rows.shape
    docs_dev, dlen = (slabs.shape[0], slabs.shape[1])
    per = wanted.shape[2]
    group = math.gcd(sources, 16)
    token_ids = jnp.arange(dlen, dtype=jnp.int32)
    alive = token_ids[None, :] < doc_lengths[:, None]
    doc_ids = jnp.arange(docs_dev, dtype=jnp.int32)
    row_blocks = rows.reshape(sources // group, group * items, qlen, dim)
    want_blocks = wanted.reshape(sources // group, group * items, per)

    def one_block(block):
        block_rows, block_want = block
        dots = jnp.einsum("bik,djk->bidj", block_rows, slabs, preferred_element_type=jnp.float32)
        best = jnp.max(jnp.where(alive[None, None], dots, -1e30), axis=3)
        totals = jnp.sum(best, axis=1) / qlen
        match = block_want[:, :, None] == doc_ids[None, None, :]
        return jnp.sum(jnp.where(match, totals[:, None, :], 0.0), axis=2)

    result = lax.map(one_block, (row_blocks, want_blocks))
    return result.reshape(sources, items, per)


def body(queries, candidates, doc_map, slabs, doc_lengths):
    q_dev, qlen, dim = queries.shape
    docs_dev = slabs.shape[0]
    shards = lax.axis_size("docs")
    cands = candidates.shape[1]
    capacity = min(q_dev, max(2, 2 * q_dev * SPREAD // shards))
    position = jnp.take(doc_map, candidates)
    owner = position // docs_dev
    local = position % docs_dev
    shard_ids = jnp.arange(shards, dtype=jnp.int32)
    hits = jnp.any(owner[:, :, None] == shard_ids[None, None, :], axis=1)
    hit_count = hits.astype(jnp.int32)
    rank = jnp.cumsum(hit_count, axis=0) - hit_count
    seat_ids = jnp.arange(capacity, dtype=jnp.int32)
    select = hits[None, :, :] & (rank[None, :, :] == seat_ids[:, None, None])
    onehot = select.astype(jnp.bfloat16)
    outgoing = jnp.einsum(
        "cjs,jik->scik", onehot, queries, preferred_element_type=jnp.float32
    ).astype(jnp.bfloat16)
    slot = jnp.take_along_axis(rank, owner, axis=1)
    cand_ids = jnp.arange(cands, dtype=jnp.int32)
    same_owner = owner[:, :, None] == owner[:, None, :]
    earlier = cand_ids[None, :] < cand_ids[:, None]
    order = jnp.sum((same_owner & earlier[None]).astype(jnp.int32), axis=2)
    per_ids = jnp.arange(PER, dtype=jnp.int32)
    match = (owner[:, :, None, None] == shard_ids[None, None, :, None]) & (
        order[:, :, None, None] == per_ids[None, None, None, :]
    )
    listed = jnp.sum(jnp.where(match, local[:, :, None, None], 0), axis=1)
    picked = jnp.sum(jnp.where(select[:, :, :, None], listed[None], 0), axis=1)
    picked = jnp.transpose(picked, (1, 0, 2))
    arrived_rows, arrived_want = (
        lax.all_to_all(outgoing, "docs", split_axis=0, concat_axis=0, tiled=True),
        lax.all_to_all(picked, "docs", split_axis=0, concat_axis=0, tiled=True),
    )
    result = score_items(arrived_rows, arrived_want, slabs, doc_lengths)
    answers = lax.all_to_all(result, "docs", split_axis=0, concat_axis=0, tiled=True)
    flat_index = (owner * capacity + slot) * PER + order
    return jnp.take(answers.reshape(-1), flat_index)


NCH = 2
MESH = pl.DeviceIdType.MESH


def gather_score_kernel(q_ref, slab_ref, len_hbm, cand_hbm, map_hbm, out_ref, held, docs, best, parts, table,
                        len_ref, cand_ref, map_ref, send_sem, recv_sem, back_send, back_recv, load_sem):
    me = lax.axis_index("docs")
    z, x = me // 2, me % 2
    h = z // 2
    mate = z * 2 + (1 - x)
    rows = q_ref.shape[0]
    step_rows = rows // NCH
    n_docs, dlen, dim = slab_ref.shape
    shards = held.shape[0]
    loads = [
        pltpu.make_async_copy(src, dst, load_sem.at[i])
        for i, (src, dst) in enumerate((
            (slab_ref, docs), (len_hbm, len_ref), (q_ref, held.at[me]), (cand_hbm, cand_ref), (map_hbm, map_ref)))
    ]
    middle = jnp.logical_or(z == 1, z == 2)

    barrier = pltpu.get_barrier_semaphore()
    for k in range(1, shards):
        pl.semaphore_signal(barrier, inc=1, device_id={"docs": (me + k) % shards}, device_id_type=MESH)
    for load in loads:
        load.start()
    pl.semaphore_wait(barrier, shards - 1)

    def chunk(c):
        return pl.ds(c * step_rows, step_rows)

    def link(source, origin, c, kind, target):
        return pltpu.make_async_remote_copy(
            src_ref=source.at[chunk(c)],
            dst_ref=held.at[origin, chunk(c)],
            send_sem=send_sem.at[kind * NCH + c],
            recv_sem=recv_sem.at[origin * NCH + c],
            device_id={"docs": target},
            device_id_type=MESH,
        )

    inner = (z + 1 - 2 * h) * 2 + x
    outer = jnp.where(middle, z - 1 + 2 * h, 1 + h) * 2 + x
    for c in range(NCH):
        link(q_ref, me, c, 0, inner).start()
        link(q_ref, me, c, 1, mate).start()

        @pl.when(middle)
        def _(c=c):
            link(q_ref, me, c, 2, outer).start()

    loads[0].wait()
    loads[1].wait()

    def mask_doc(d, carry):
        rows_d = docs[d].astype(jnp.float32)
        live = lax.broadcasted_iota(jnp.int32, (dlen, dim), 0) < len_ref[d]
        docs[d] = jnp.where(live, rows_d, rows_d[0:1]).astype(jnp.bfloat16)
        return carry

    lax.fori_loop(0, n_docs, mask_doc, 0, unroll=2)

    col_q = lax.broadcasted_iota(jnp.int32, (16, rows), 1) // 32
    row_q = lax.broadcasted_iota(jnp.int32, (16, rows), 0)
    pick = jnp.where(col_q == row_q, 1.0, 0.0).astype(jnp.bfloat16)
    G = 8

    def half(origin, c):
        q = held[origin, chunk(c)]

        def group(g, carry):
            block = docs[pl.ds(g * G, G)].reshape(G * dlen, dim)
            dots = lax.dot_general(block, q, (((1,), (1,)), ((), ())), preferred_element_type=jnp.float32)
            best[pl.ds(pl.multiple_of(g * G, G), G), chunk(c)] = jnp.max(
                dots.reshape(G, dlen, step_rows), axis=1)
            return carry

        lax.fori_loop(0, n_docs // G, group, 0, unroll=True)

    def total():
        full = best[...]
        hi = full.astype(jnp.bfloat16)
        rest = full - hi.astype(jnp.float32)
        mid = rest.astype(jnp.bfloat16)
        low = (rest - mid.astype(jnp.float32)).astype(jnp.bfloat16)
        stacked = jnp.concatenate([hi, mid, low, jnp.zeros_like(hi)], axis=0)
        summed = lax.dot_general(pick, stacked, (((1,), (1,)), ((), ())), preferred_element_type=jnp.float32)
        return summed

    def back(origin):
        return pltpu.make_async_remote_copy(
            src_ref=parts.at[origin],
            dst_ref=table.at[me],
            send_sem=back_send.at[origin],
            recv_sem=back_recv.at[me],
            device_id={"docs": origin},
            device_id_type=MESH,
        )

    def answer(origin):
        parts[origin] = total()
        back(origin).start()

    def arrive(origin, c):
        link(held.at[origin], origin, c, 0, mate).wait_recv()

    column = (1 - z + 4 * h, 2 - h, 3 - 3 * h)
    onward = jnp.where(middle, 3 - z, mate // 2), jnp.where(middle, 3 * h, mate // 2), jnp.where(middle, 3 * h, mate // 2)

    def relay(p, c, go=True):
        origin = column[p] * 2 + x
        target = jnp.where(middle, onward[p] * 2 + x, mate)
        if go:
            arrive(origin, c)

        side = link(held.at[origin], origin, c, 4 + 2 * p, mate)
        ahead = link(held.at[origin], origin, c, 3 + 2 * p, target)

        @pl.when(middle)
        def _():
            ahead.start() if go else ahead.wait_send()

        side.start() if go else side.wait_send()

    near = [column[p] * 2 + x for p in range(3)]
    far = [column[p] * 2 + 1 - x for p in range(3)]

    loads[2].wait()
    half(me, 0)
    relay(0, 0)
    half(me, 1)
    table[me] = total()
    relay(0, 1)
    half(near[0], 0)
    half(near[0], 1)
    answer(near[0])
    arrive(mate, 0)
    half(mate, 0)
    relay(1, 0)
    arrive(mate, 1)
    relay(1, 1)
    half(mate, 1)
    answer(mate)
    half(near[1], 0)
    half(near[1], 1)
    answer(near[1])
    relay(2, 0)
    arrive(far[0], 0)
    half(far[0], 0)
    relay(2, 1)
    arrive(far[0], 1)
    half(far[0], 1)
    answer(far[0])
    half(near[2], 0)
    half(near[2], 1)
    answer(near[2])
    for p in (1, 2):
        for c in range(NCH):
            arrive(far[p], c)
            half(far[p], c)
        answer(far[p])

    for c in range(NCH):
        link(q_ref, me, c, 0, inner).wait_send()
        link(q_ref, me, c, 1, mate).wait_send()

        @pl.when(middle)
        def _(c=c):
            link(q_ref, me, c, 2, outer).wait_send()
    for p in range(3):
        for c in range(NCH):
            relay(p, c, False)
    for k in range(1, shards):
        other = (me + k) % shards
        back(other).wait_send()
        pltpu.make_async_remote_copy(
            src_ref=parts.at[other], dst_ref=table.at[other], send_sem=back_send.at[other],
            recv_sem=back_recv.at[other], device_id={"docs": other}, device_id_type=MESH,
        ).wait_recv()
    loads[3].wait()
    loads[4].wait()
    cand = cand_ref[...]
    items, cands = cand.shape
    lanes = 128
    cand = jnp.concatenate([cand, cand], axis=1)
    low = cand % lanes
    position = jnp.zeros_like(cand)
    for b in range(map_ref.shape[1] // lanes):
        piece = jnp.broadcast_to(map_ref[:, b * lanes:(b + 1) * lanes], (items, lanes))
        got = jnp.take_along_axis(piece, low, axis=1)
        position = jnp.where(cand // lanes == b, got, position)
    owner, local = position // 32, position % 32
    out = jnp.zeros((items, lanes), jnp.float32)
    for o in range(shards):
        part = table[o]
        got = (jnp.take_along_axis(part, local, axis=1) + jnp.take_along_axis(part, local + 32, axis=1)
               + jnp.take_along_axis(part, local + 64, axis=1))
        out = jnp.where(owner == o, got, out)
    out_ref[...] = out[:, :cands]


def dense_body(queries, candidates, doc_map, slabs, doc_lengths):
    q_dev, qlen, dim = queries.shape
    shards = lax.axis_size("docs")
    rows = q_dev * qlen
    vmem = pl.BlockSpec(memory_space=pltpu.VMEM)
    hbm = pl.BlockSpec(memory_space=pl.ANY)
    scores = pl.pallas_call(
        gather_score_kernel,
        out_shape=jax.ShapeDtypeStruct(candidates.shape, jnp.float32),
        in_specs=[hbm] * 5,
        out_specs=vmem,
        scratch_shapes=[
            pltpu.VMEM((shards, rows, dim), jnp.bfloat16),
            pltpu.VMEM(slabs.shape, jnp.bfloat16),
            pltpu.VMEM((slabs.shape[0], rows), jnp.float32),
            pltpu.VMEM((shards, q_dev, 128), jnp.float32),
            pltpu.VMEM((shards, q_dev, 128), jnp.float32),
            pltpu.SMEM(doc_lengths.shape, jnp.int32),
            pltpu.VMEM(candidates.shape, jnp.int32),
            pltpu.VMEM((1,) + doc_map.shape, jnp.int32),
            pltpu.SemaphoreType.DMA((9 * NCH,)),
            pltpu.SemaphoreType.DMA((shards * NCH,)),
            pltpu.SemaphoreType.DMA((shards,)),
            pltpu.SemaphoreType.DMA((shards,)),
            pltpu.SemaphoreType.DMA((5,)),
        ],
        compiler_params=pltpu.CompilerParams(
            collective_id=0, has_side_effects=True, vmem_limit_bytes=60 * 1024 * 1024
        ),
        name="gather_score",
    )(queries.reshape(rows, dim), slabs, doc_lengths, candidates, doc_map.reshape(1, -1))
    return scores * (1.0 / qlen)


def any_body(queries, candidates, doc_map, slabs, doc_lengths):
    sizes = (queries.shape, candidates.shape, slabs.shape, lax.axis_size("docs"))
    if sizes == ((16, 32, 128), (16, 64), (32, 128, 128), 8):
        return dense_body(queries, candidates, doc_map, slabs, doc_lengths)
    return body(queries, candidates, doc_map, slabs, doc_lengths)


def solution(mesh):
    placed = (
        P(("groups", "docs", "rep"), None, None),
        P(("groups", "docs", "rep"), None),
        P("groups"),
        P(("groups", "docs"), None, None),
        P(("groups", "docs")),
    )
    return jax.shard_map(
        any_body,
        mesh=mesh,
        in_specs=placed,
        out_specs=P(("groups", "docs", "rep"), None),
        check_vma=False,
    )
```
